32 devices in a mesh: comp: 2 (over x), row: 4 (over z), col: 4 (over y, core).
Axes of the slice: x: 2, y: 2, z: 4, core: 2. Of those that a mesh axis runs over, the one named last changes fastest.
Arguments:
- column: float32 [2, 8, 128, 512], P('comp', None, 'row', 'col'), may hold values from -6 to 6
- fast_state: float32 [2, 3, 128, 512], P('comp', None, 'row', 'col'), may hold values from -6 to 6
- wave_depth: float32 [2, 128, 512], P('comp', 'row', 'col'), may hold values from 0.5 to 2
- wet_mask: int32 [2, 128, 512], P('comp', 'row', 'col'), may hold values 0 or 1
- surface: float32 [2, 8, 128, 512], P('comp', None, 'row', 'col'), may hold values from -6 to 6
- coupling: float32 [2, 11, 8], P('comp'), may hold values from -2 to 2
- emission: float32 [2, 8, 11], P('comp'), may hold values from -1.75 to 1.75
- remap_weight: bfloat16 [2, 128, 16, 4, 128], P('comp', 'row', 'col'), may hold values from -1.5 to 1.5
- send_block: int32 [2, 4, 16, 32], P('comp', 'row', 'col'), may hold values from 0 to 31
- link_slot: int32 [2, 4, 512], P('comp', 'row', 'col'), may hold values from 0 to 127, as said below
Outputs:
- new_column: float32 [2, 8, 128, 512], P('comp', None, 'row', 'col')
- fast_final: float32 [2, 3, 128, 512], P('comp', None, 'row', 'col')
- next_surface: float32 [2, 8, 128, 512], P('comp', None, 'row', 'col')
The draws below stay inside these ranges and needn't reach their ends.
Inputs may be any that keep to these rules, and one draw needn't show every extreme that they name: `send_block`: each entry names a latitude row of the sending device's tile. `link_slot`: on each device the 128 links read every received slot exactly once.
All inputs are finite; a program needn't handle non-finite values. No bound on the sum of `wet_mask` on one device may be relied on, other than what follows from the above.
Results may differ from the reference program's by a relative error of at most 0.0023.
Values may be sent and summed in bfloat16 or wider, within the bound.
A program may use at most 64 MiB of HBM per device.

```python
import math
import jax
import jax.numpy as jnp
from jax import lax

H = 32
W = 128
K = 4
SPAN = 4
Q = 8
L = 8
SUBSTEPS = 32
BANDS = 4
PEERS = 4
SLOTS = 32
NY = 128
NX = 512


def draw_link_slot(key, part):
    key = jax.random.fold_in(key, 7)
    ordering = jnp.broadcast_to(jnp.arange(H * K, dtype=jnp.int32), (2, BANDS, PEERS, H * K))
    shuffled = jax.random.permutation(key, ordering, axis=3, independent=True)
    return shuffled.reshape(2, BANDS, PEERS * H * K)


def touch_ends(drawn, key, least, top_value):
    longest = drawn.shape.index(max(drawn.shape))
    spots = []
    for shift in (0, 1):
        where = [jax.random.randint(jax.random.fold_in(key, axis), (), 0, length) for axis, length in enumerate(drawn.shape)]
        where[longest] = (where[longest] + shift) % drawn.shape[longest]
        spots.append(tuple(where))
    return drawn.at[spots[0]].set(least).at[spots[1]].set(top_value)


def level_of(own_key, shape, pieces, low, largest):
    factor_of = 1.0
    for axis_at, parts in pieces:
        heights = jax.random.uniform(jax.random.fold_in(jax.random.fold_in(own_key, 6), axis_at), (parts,), jnp.float32, low / len(pieces), largest / len(pieces))
        factor_of = factor_of * jnp.repeat(jnp.exp(heights), shape[axis_at] // parts).reshape((-1,) + (1,) * (len(shape) - 1 - axis_at))
    return factor_of


def normal_values(own_key, shape, deviation, reach, split=(), held_as=jnp.bfloat16):
    level = level_of(own_key, shape, split, -0.22, 0.18) if split else 1.0
    values = jax.random.normal(own_key, shape, jnp.float32) * deviation * level
    return jnp.minimum(jnp.maximum(values, -reach), reach).astype(held_as)


def setup_inputs(seed: int = 0) -> dict:
    keys = jax.random.split(jax.random.key(seed), 11)
    return {
        "column": normal_values(keys[0], (2, L, NY, NX), 1.0, 6.0, ((0, 2), (2, 4), (3, 4)), jnp.float32),
        "fast_state": normal_values(keys[1], (2, 3, NY, NX), 1.0, 6.0, ((0, 2), (2, 4), (3, 4)), jnp.float32),
        "wave_depth": jnp.clip(jnp.exp(math.log(2.0) - 1.3862944 * jax.random.uniform(keys[2], (2, NY, NX), jnp.float32) ** level_of(keys[2], (2, NY, NX), ((0, 2), (1, 4), (2, 4)), -0.2, 0.2)), 0.5, 2.0),
        "wet_mask": touch_ends((jax.random.randint(keys[3], (2, NY, NX), 0, 4) < 3).astype(jnp.int32), jax.random.fold_in(keys[3], 1), 0, 1),
        "surface": normal_values(keys[4], (2, Q, NY, NX), 1.0, 6.0, ((0, 2), (2, 4), (3, 4)), jnp.float32),
        "coupling": normal_values(keys[5], (2, L + 3, Q), Q ** -0.5, 2.0, ((0, 2),), jnp.float32),
        "emission": normal_values(keys[6], (2, Q, L + 3), (L + 3) ** -0.5, 1.75, ((0, 2),), jnp.float32),
        "remap_weight": normal_values(keys[7], (2, NY, K * PEERS, SPAN, W), (K * SPAN) ** -0.5, 1.5, ((0, 2), (1, 4), (2, 4))),
        "send_block": touch_ends(jax.random.randint(keys[8], (2, BANDS, PEERS * PEERS, SLOTS), 0, H), jax.random.fold_in(keys[8], 1), 0, H - 1).astype(jnp.int32),
        "link_slot": draw_link_slot(jax.random.fold_in(keys[10], 71), 0),
    }


STEP_SIZE = 0.35
DAMPING = 0.97


def pick_rows(table, index):
    return table[index]


def remap(outgoing, chosen, linked_slots, weights):
    blocks = outgoing.reshape(Q, BANDS, H, PEERS, W).transpose(1, 3, 2, 0, 4)
    chosen = chosen.reshape(BANDS, PEERS, PEERS * SLOTS)
    payload = jax.vmap(jax.vmap(pick_rows))(blocks, chosen)
    payload = payload.reshape(BANDS, PEERS, PEERS, SLOTS, Q, W).transpose(0, 2, 1, 3, 4, 5)
    arrived = payload.reshape(BANDS, PEERS, PEERS * SLOTS, Q, W)
    linked = jax.vmap(jax.vmap(pick_rows))(arrived, linked_slots.reshape(BANDS, PEERS, H * K))
    linked = linked.reshape(BANDS, PEERS, H, K, Q, W)
    weights = weights.reshape(BANDS, H, PEERS, K, SPAN, W).transpose(0, 2, 1, 3, 4, 5)

    def one_band(paired):
        values, matrices = paired
        values = values.astype(jnp.float32)
        matrices = matrices.astype(jnp.float32)
        total = jnp.zeros((PEERS, H, Q, W), jnp.float32)
        for offset in range(SPAN):
            shifted = jnp.roll(values, SPAN // 2 - offset, axis=4)
            total = total + jnp.sum(shifted * matrices[:, :, :, offset][:, :, :, None, :], axis=2)
        return total

    mapped = lax.map(one_band, (linked, weights))
    return mapped.transpose(3, 0, 2, 1, 4).reshape(Q, BANDS * H, PEERS * W)


def fast_substep(height, east_flow, north_flow, depth_field, wet_float, pushes):
    flux_east = depth_field * east_flow
    flux_north = depth_field * north_flow
    west_flux = jnp.roll(flux_east, 1, axis=1)
    south_flux = jnp.pad(flux_north, ((1, 0), (0, 0)))[:-1]
    height_next = height - STEP_SIZE * ((flux_east - west_flux) + (flux_north - south_flux)) + pushes[0]
    east_height = jnp.roll(height_next, -1, axis=1)
    north_height = jnp.pad(height_next, ((0, 1), (0, 0)))[1:]
    east_next = wet_float * (DAMPING * east_flow - STEP_SIZE * (east_height - height_next) + pushes[1])
    north_next = wet_float * (DAMPING * north_flow - STEP_SIZE * (north_height - height_next) + pushes[2])
    return height_next, east_next, north_next


def reference(column, fast_state, wave_depth, wet_mask, surface, coupling, emission, remap_weight, send_block, link_slot):
    wet_all = wet_mask.astype(jnp.float32)
    outgoing = (surface * wet_all[:, None]).astype(jnp.bfloat16)
    per_substep = 1.0 / SUBSTEPS
    columns, finals, surfaces = [], [], []
    for target in range(2):
        source = 1 - target
        forcing = remap(outgoing[source], send_block[source], link_slot[target], remap_weight[target])
        driving = jnp.einsum('mq,qyx->myx', coupling[target], forcing, precision=lax.Precision.HIGHEST)
        updated = column[target] + driving[:L]
        pushes = driving[L:] * per_substep
        height, east_flow, north_flow = fast_state[target, 0], fast_state[target, 1], fast_state[target, 2]
        totals = jnp.zeros((3, NY, NX), jnp.float32)
        for index in range(SUBSTEPS):
            height, east_flow, north_flow = fast_substep(height, east_flow, north_flow, wave_depth[target],
                                                         wet_all[target], pushes)
            totals = totals + jnp.stack([height, east_flow, north_flow])
        fields = jnp.concatenate([updated, totals * per_substep], 0)
        emitted = jnp.tanh(jnp.einsum('qm,myx->qyx', emission[target], fields, precision=lax.Precision.HIGHEST))
        columns.append(updated)
        finals.append(jnp.stack([height, east_flow, north_flow]))
        surfaces.append(emitted)
    return jnp.stack(columns), jnp.stack(finals), jnp.stack(surfaces)
```

```python
import functools

import jax
import jax.numpy as jnp
from jax import lax
from jax.experimental import pallas as pl
from jax.experimental.pallas import tpu as pltpu
from jax.sharding import PartitionSpec as P

H = 32
W = 128
K = 4
SPAN = 4
Q = 8
L = 8
SUBSTEPS = 32
FAST = 3
STEP_SIZE = 0.35
DAMPING = 0.97
CHUNKS = 2
PART = 32
ROWS = 3 * H
MESH = pl.DeviceIdType.MESH
TURNS = [(dr, dc) for dr in (-1, 0, 1) for dc in (-1, 0, 1) if (dr, dc) != (0, 0)]


def table_rows(peers):
    return max(16, -(-peers // 16) * 16)


def mask_order(peers):
    bits = peers.bit_length() - 1
    return sorted(range(peers), key=lambda m: int(format(m, "b").zfill(bits)[::-1], 2))


def lower_bits(mask, peers):
    bits = [1 << b for b in reversed(range(peers.bit_length() - 1))]
    return [b for b in bits if mask == 0 or b < (mask & -mask)]


def kernel(
    peers,
    bands,
    column,
    fast_state,
    depth,
    wet_mask,
    surface,
    coupling,
    emission,
    weights,
    send_block,
    link_slot,
    new_column,
    fast_final,
    next_surface,
    mine,
    got,
    table,
    wide,
    turned,
    linked,
    forcing,
    field_a,
    field_e,
    field_w,
    edge_e,
    edge_w,
    push_a,
    push_e,
    push_w,
    pedge_e,
    pedge_w,
    wave,
    fixed,
    totals,
    block_send,
    block_recv,
    field_send,
    field_recv,
    push_send,
    push_recv,
):
    comp = lax.axis_index("comp")
    row = lax.axis_index("row")
    col = lax.axis_index("col")
    slots = send_block.shape[1]
    head = table_rows(peers)
    bits = peers.bit_length() - 1
    up_ok = row < bands - 1
    down_ok = row > 0

    def at(dr, dc):
        return {"row": row + dr, "col": lax.rem(col + dc + peers, peers)}

    def reaches(dr):
        return up_ok if dr > 0 else down_ok

    def guarded(dr, act):
        if dr == 0:
            act()
        else:
            pl.when(reaches(dr))(act)

    barrier = pltpu.get_barrier_semaphore()

    def greet(device):
        pl.semaphore_signal(barrier, inc=1, device_id=device, device_id_type=MESH)

    greet({"comp": 1 - comp})
    for b in range(bits):
        greet({"col": col ^ (1 << b)})
    for dr, dc in TURNS:
        guarded(dr, functools.partial(greet, at(dr, dc)))

    wet = wet_mask[...].astype(jnp.float32)
    table[...] = jnp.zeros_like(table)
    table[0:peers, 0:slots] = send_block[...].astype(jnp.float32)
    mine[0:head] = table[...].astype(jnp.bfloat16)
    for q in range(Q):
        mine[head + q * H : head + (q + 1) * H] = (surface[q] * wet).astype(jnp.bfloat16)

    lane = lax.broadcasted_iota(jnp.int32, (H, W), 1)

    def pack(fields, east, west, tile):
        low = jnp.zeros((H, W), jnp.float32)
        high = jnp.zeros((H, W), jnp.float32)
        for i, cells in enumerate(fields):
            here = (lane >= i * PART) & (lane < (i + 1) * PART)
            first = cells if i == 0 else pltpu.roll(cells, i * PART, 1)
            turn = (i * PART - (W - PART)) % W
            last = cells if turn == 0 else pltpu.roll(cells, turn, 1)
            low = jnp.where(here, first, low)
            high = jnp.where(here, last, high)
        west[tile] = low
        east[tile] = high

    own = slice(H, 2 * H)
    statics = [fast_state[i] for i in range(FAST)] + [depth[...], wet]
    for i, cells in enumerate(statics):
        field_a[i, own] = cells
    pack(statics[:4], edge_e, edge_w, 0)
    pack(statics[4:], edge_e, edge_w, 1)

    @pl.when(jnp.logical_not(down_ok))
    def _():
        for ref in (field_a, field_e, field_w, push_a, push_e, push_w):
            ref[:, 0:H] = jnp.zeros_like(ref[:, 0:H])

    @pl.when(jnp.logical_not(up_ok))
    def _():
        for ref in (field_a, field_e, field_w, push_a, push_e, push_w):
            ref[:, 2 * H : 3 * H] = jnp.zeros_like(ref[:, 2 * H : 3 * H])

    beyond = up_ok.astype(jnp.int32) + down_ok.astype(jnp.int32)
    pl.semaphore_wait(barrier, 1 + bits + 2 + 3 * beyond)

    chunk_rows = Q * H // CHUNKS

    def span_of(chunk):
        if chunk == 0:
            return pl.ds(0, head + chunk_rows)
        return pl.ds(head + chunk * chunk_rows, chunk_rows)

    def block_copy(mask, bit, chunk):
        source = col ^ mask
        index = (mask | bit) * CHUNKS + chunk
        return pltpu.make_async_remote_copy(
            src_ref=got.at[source, span_of(chunk)],
            dst_ref=got.at[source, span_of(chunk)],
            send_sem=block_send.at[index],
            recv_sem=block_recv.at[index],
            device_id={"col": col ^ bit},
            device_id_type=MESH,
        )

    def arrival(mask, chunk):
        source = col ^ mask
        index = mask * CHUNKS + chunk
        if mask == 0:
            return pltpu.make_async_remote_copy(
                src_ref=mine.at[span_of(chunk)],
                dst_ref=got.at[col, span_of(chunk)],
                send_sem=block_send.at[index],
                recv_sem=block_recv.at[index],
                device_id={"comp": 1 - comp},
                device_id_type=MESH,
            )
        bit = mask & -mask
        return pltpu.make_async_remote_copy(
            src_ref=got.at[source, span_of(chunk)],
            dst_ref=got.at[source, span_of(chunk)],
            send_sem=block_send.at[index],
            recv_sem=block_recv.at[index],
            device_id={"col": col ^ bit},
            device_id_type=MESH,
        )

    def halo_copy(dr, dc, middle, east, west, land_e, land_w, send, recv):
        index = TURNS.index((dr, dc))
        land = pl.ds(H - H * dr, H)
        if dc == 0:
            src, dst = middle.at[:, pl.ds(H, H)], middle.at[:, land]
        elif dc > 0:
            src, dst = east, land_w.at[:, land]
        else:
            src, dst = west, land_e.at[:, land]
        return pltpu.make_async_remote_copy(
            src_ref=src,
            dst_ref=dst,
            send_sem=send.at[index],
            recv_sem=recv.at[index],
            device_id=at(dr, dc),
            device_id_type=MESH,
        )

    field_halo = (field_a, edge_e, edge_w, field_e, field_w, field_send, field_recv)
    push_halo = (push_a, pedge_e, pedge_w, push_e, push_w, push_send, push_recv)

    def send_halo(halo):
        for dr, dc in TURNS:
            guarded(dr, lambda dr=dr, dc=dc: halo_copy(dr, dc, *halo).start())

    def await_halo(halo):
        for dr, dc in TURNS:
            guarded(-dr, lambda dr=dr, dc=dc: halo_copy(dr, dc, *halo).wait_recv())

    def drain_halo(halo):
        for dr, dc in TURNS:
            guarded(dr, lambda dr=dr, dc=dc: halo_copy(dr, dc, *halo).wait_send())

    for chunk in range(CHUNKS):
        arrival(0, chunk).start()
    send_halo(field_halo)

    wide[...] = weights[...].astype(jnp.float32)
    for k in range(K):
        for d in range(SPAN):
            plane = wide[pl.ds(k * SPAN + d, H, stride=K * SPAN), :]
            turn = (d - SPAN // 2) % W
            turned[k * SPAN + d] = plane if turn == 0 else pltpu.roll(plane, turn, 1)

    links = H * K
    rows_l = lax.broadcasted_iota(jnp.int32, (links, links), 0)
    lanes_l = lax.broadcasted_iota(jnp.int32, (links, links), 1)

    def hot(condition):
        return jnp.where(condition, 1.0, 0.0).astype(jnp.bfloat16)

    def dot_nt(a, b):
        return lax.dot_general(
            a, b, (((1,), (1,)), ((), ())), preferred_element_type=jnp.float32
        )

    order = hot(lanes_l == (rows_l & (H - 1)) * K + (rows_l >> 5))
    by_slot = hot(rows_l == link_slot[...])
    slot_of_link = dot_nt(order, by_slot).astype(jnp.bfloat16)

    waited = []
    order_of = mask_order(peers)
    senders = [m for m in order_of if m == 0 or lower_bits(m, peers)]
    leaves = [m for m in order_of if m not in senders]

    def receive(mask, chunk):
        arrival(mask, chunk).wait_recv()
        for bit in lower_bits(mask, peers):
            block_copy(mask, bit, chunk).start()

    for mask in senders:
        for chunk in range(CHUNKS):
            receive(mask, chunk)
    pick = None
    per_chunk = Q // CHUNKS
    for chunk in range(CHUNKS):
        for mask in leaves:
            receive(mask, chunk)
        if chunk == 0:
            pieces = []
            rows_h = lax.broadcasted_iota(jnp.int32, (H, W), 0)
            rows_t = lax.broadcasted_iota(jnp.int32, (head, W), 0)
            for s in range(peers):
                listed = got[s, 0:head].astype(jnp.float32)
                chosen = jnp.sum(jnp.where(rows_t == col, listed, 0.0), axis=0, keepdims=True)
                chosen = jnp.broadcast_to(chosen, (H, W)).astype(jnp.int32)
                turn = s * slots % W
                chosen = chosen if turn == 0 else pltpu.roll(chosen, turn, 1)
                here = (lane >= s * slots) & (lane < (s + 1) * slots)
                pieces.append(hot(here & (chosen == rows_h)))
            block_of_slot = jnp.concatenate(pieces, axis=0)
            pick = dot_nt(slot_of_link, block_of_slot).astype(jnp.bfloat16)
        for pair in range(per_chunk // 2):
            first = chunk * per_chunk + 2 * pair
            cells = []
            for q in (first, first + 1):
                tall = got[:, head + q * H : head + (q + 1) * H, :]
                cells.append(tall.reshape(peers * H, W))
            linked[...] = jnp.dot(
                pick, jnp.concatenate(cells, axis=1), preferred_element_type=jnp.float32
            )
            for side in range(2):
                total = jnp.zeros((H, W), jnp.float32)
                for d in range(SPAN):
                    part = jnp.zeros((H, W), jnp.float32)
                    for k in range(K):
                        part = part + (
                            linked[k * H : (k + 1) * H, side * W : (side + 1) * W]
                            * turned[k * SPAN + d]
                        )
                    turn = (SPAN // 2 - d) % W
                    total = total + (part if turn == 0 else pltpu.roll(part, turn, 1))
                forcing[first + side] = total

    def driven(m, rows):
        total = coupling[0, m] * forcing[0, rows]
        for q in range(1, Q):
            total = total + coupling[q, m] * forcing[q, rows]
        return total

    everywhere = slice(0, H)
    pushes = [driven(L + i, everywhere) * (1.0 / SUBSTEPS) for i in range(FAST)]
    for i in range(FAST):
        push_a[i, own] = pushes[i]
    pack(pushes, pedge_e, pedge_w, 0)
    send_halo(push_halo)

    for m in range(L):
        new_column[m] = column[m] + driven(m, everywhere)
    for q in range(Q):
        total = emission[q, 0] * new_column[0]
        for m in range(1, L):
            total = total + emission[q, m] * new_column[m]
        next_surface[q] = total
    await_halo(field_halo)

    lane_r = lax.broadcasted_iota(jnp.int32, (ROWS, W), 1)

    def beside(east, west, i):
        tile, place = divmod(i, W // PART)
        near = east[tile]
        near = near if place == 0 else pltpu.roll(near, (W - place * PART) % W, 1)
        turn = (W - PART - place * PART) % W
        far = west[tile]
        far = far if turn == 0 else pltpu.roll(far, turn, 1)
        cells = jnp.where(lane_r < PART, near, 0.0)
        return jnp.where(lane_r >= W - PART, far, cells)

    scale = [STEP_SIZE, 1.0, 1.0, STEP_SIZE * STEP_SIZE, 1.0]
    for i in range(5):
        ref = wave.at[i] if i < FAST else fixed.at[i - FAST]
        ref[0] = field_a[i] * scale[i]
        ref[1] = beside(field_e, field_w, i) * scale[i]
    totals[...] = jnp.zeros_like(totals)
    await_halo(push_halo)
    pscale = [STEP_SIZE, 1.0, 1.0]
    for i in range(FAST):
        fixed[2 + i, 0] = push_a[i] * pscale[i]
        fixed[2 + i, 1] = beside(push_e, push_w, i) * pscale[i]

    lane8 = lax.broadcasted_iota(jnp.int32, (8, W), 1)
    sub8 = lax.broadcasted_iota(jnp.int32, (8, W), 0)
    west_rim = lane8 == 0
    east_rim = lane8 == W - 1
    south_rim = sub8 == 0
    north_rim = sub8 == 7
    top = jnp.where(up_ok, 1.0, 0.0).astype(jnp.float32)

    def sweep(low, high):
        south_prev = [jnp.zeros((8, W), jnp.float32)] * 2
        held = None
        for block in range(low, high + 2):
            rows = slice(8 * block, 8 * block + 8)
            now = None
            if block <= high:
                flow_e = [wave[1, t, rows] for t in range(2)]
                flow_n = [wave[2, t, rows] for t in range(2)]
                deep = [fixed[0, t, rows] for t in range(2)]
                flux_e = [deep[t] * flow_e[t] for t in range(2)]
                flux_n = [deep[t] * flow_n[t] for t in range(2)]
                spun = [pltpu.roll(flux_e[t], 1, 0 + 1) for t in range(2)]
                lifted = [pltpu.roll(flux_n[t], 1, 0) for t in range(2)]
                high_new = []
                for t in range(2):
                    from_west = jnp.where(west_rim, spun[1 - t], spun[t])
                    from_south = jnp.where(south_rim, south_prev[t], lifted[t])
                    level = (
                        wave[0, t, rows]
                        - ((flux_e[t] - from_west) + (flux_n[t] - from_south))
                        + fixed[2, t, rows]
                    )
                    if block == 2 * H // 8:
                        level = level * top
                    wave[0, t, rows] = level
                    high_new.append(level)
                if 4 <= block < 8:
                    orows = slice(8 * block - H, 8 * block - H + 8)
                    totals[0, orows] += high_new[0]
                south_prev = lifted
                down = [pltpu.roll(high_new[t], 7, 0) for t in range(2)]
                now = (rows, block, high_new, flow_e, flow_n, down)
            if held is not None:
                rows, block_h, level, flow_e, flow_n, down = held
                spun = [pltpu.roll(level[t], W - 1, 1) for t in range(2)]
                for t in range(2):
                    to_east = jnp.where(east_rim, spun[1 - t], spun[t])
                    if now is None:
                        to_north = down[t]
                    else:
                        to_north = jnp.where(north_rim, now[5][t], down[t])
                    open_cells = fixed[1, t, rows]
                    east = open_cells * (
                        DAMPING * flow_e[t] - (to_east - level[t]) + fixed[3, t, rows]
                    )
                    north = open_cells * (
                        DAMPING * flow_n[t] - (to_north - level[t]) + fixed[4, t, rows]
                    )
                    wave[1, t, rows] = east
                    wave[2, t, rows] = north
                    if t == 0 and 4 <= block_h < 8:
                        orows = slice(8 * block_h - H, 8 * block_h - H + 8)
                        totals[1, orows] += east
                        totals[2, orows] += north
            held = now

    for group in range(SUBSTEPS // 8):

        def step(_, carry, group=group):
            sweep(group, ROWS // 8 - 1 - group)
            return carry

        lax.fori_loop(0, 8, step, 0)

    back = [1.0 / STEP_SIZE, 1.0, 1.0]
    for i in range(FAST):
        fast_final[i] = wave[i, 0, own] * back[i]
    mean = [totals[i] * (back[i] / SUBSTEPS) for i in range(FAST)]
    for q in range(Q):
        total = next_surface[q]
        for i in range(FAST):
            total = total + emission[q, L + i] * mean[i]
        next_surface[q] = jnp.tanh(total)

    for chunk in range(CHUNKS):
        for mask in range(peers):
            arrival(mask, chunk).wait_send()
    drain_halo(field_halo)
    drain_halo(push_halo)


def solution(mesh):
    peers = mesh.shape["col"]
    bands = mesh.shape["row"]
    head = table_rows(peers)

    def body(
        column,
        fast_state,
        wave_depth,
        wet_mask,
        surface,
        coupling,
        emission,
        remap_weight,
        send_block,
        link_slot,
    ):
        f32 = jnp.float32
        vmem = pl.BlockSpec(memory_space=pltpu.VMEM)
        smem = pl.BlockSpec(memory_space=pltpu.SMEM)
        dma = pltpu.SemaphoreType.DMA
        outs = pl.pallas_call(
            functools.partial(kernel, peers, bands),
            out_shape=(
                jax.ShapeDtypeStruct((L, H, W), f32),
                jax.ShapeDtypeStruct((FAST, H, W), f32),
                jax.ShapeDtypeStruct((Q, H, W), f32),
            ),
            in_specs=[vmem] * 5 + [smem] * 2 + [vmem] * 3,
            out_specs=(vmem, vmem, vmem),
            scratch_shapes=[
                pltpu.VMEM((head + Q * H, W), jnp.bfloat16),
                pltpu.VMEM((peers, head + Q * H, W), jnp.bfloat16),
                pltpu.VMEM((head, W), f32),
                pltpu.VMEM((H * K * SPAN, W), f32),
                pltpu.VMEM((K * SPAN, H, W), f32),
                pltpu.VMEM((H * K, 2 * W), f32),
                pltpu.VMEM((Q, H, W), f32),
                pltpu.VMEM((5, ROWS, W), f32),
                pltpu.VMEM((2, ROWS, W), f32),
                pltpu.VMEM((2, ROWS, W), f32),
                pltpu.VMEM((2, H, W), f32),
                pltpu.VMEM((2, H, W), f32),
                pltpu.VMEM((FAST, ROWS, W), f32),
                pltpu.VMEM((1, ROWS, W), f32),
                pltpu.VMEM((1, ROWS, W), f32),
                pltpu.VMEM((1, H, W), f32),
                pltpu.VMEM((1, H, W), f32),
                pltpu.VMEM((FAST, 2, ROWS, W), f32),
                pltpu.VMEM((5, 2, ROWS, W), f32),
                pltpu.VMEM((FAST, H, W), f32),
                dma((peers * CHUNKS,)),
                dma((peers * CHUNKS,)),
                dma((8,)),
                dma((8,)),
                dma((8,)),
                dma((8,)),
            ],
            compiler_params=pltpu.CompilerParams(
                collective_id=0, has_side_effects=True, vmem_limit_bytes=40 << 20
            ),
        )(
            column[0],
            fast_state[0],
            wave_depth[0],
            wet_mask[0],
            surface[0],
            coupling[0].T,
            emission[0],
            remap_weight.reshape(H * K * SPAN, W),
            send_block[0, 0],
            link_slot[0],
        )
        return tuple(out[None] for out in outs)

    placed = (
        P("comp", None, "row", "col"),
        P("comp", None, "row", "col"),
        P("comp", "row", "col"),
        P("comp", "row", "col"),
        P("comp", None, "row", "col"),
        P("comp", None, None),
        P("comp", None, None),
        P("comp", "row", "col", None, None),
        P("comp", "row", "col", None),
        P("comp", "row", "col"),
    )
    return jax.shard_map(
        body,
        mesh=mesh,
        in_specs=placed,
        out_specs=(
            P("comp", None, "row", "col"),
            P("comp", None, "row", "col"),
            P("comp", None, "row", "col"),
        ),
        check_vma=False,
    )
```

```python
import functools

import jax
import jax.numpy as jnp
from jax import lax
from jax.experimental import pallas as pl
from jax.experimental.pallas import tpu as pltpu
from jax.sharding import PartitionSpec as P

H = 32
W = 128
K = 4
SPAN = 4
Q = 8
L = 8
SUBSTEPS = 32
FAST = 3
STEP_SIZE = 0.35
DAMPING = 0.97
CHUNKS = 2
PART = 32
ROWS = 3 * H
MESH = pl.DeviceIdType.MESH
TURNS = [(dr, dc) for dr in (-1, 0, 1) for dc in (-1, 0, 1) if (dr, dc) != (0, 0)]


def table_rows(peers):
    return max(16, -(-peers // 16) * 16)


def mask_order(peers):
    bits = peers.bit_length() - 1
    return sorted(range(peers), key=lambda m: int(format(m, "b").zfill(bits)[::-1], 2))


def lower_bits(mask, peers):
    bits = [1 << b for b in reversed(range(peers.bit_length() - 1))]
    return [b for b in bits if mask == 0 or b < (mask & -mask)]


def kernel(peers, bands, *refs):
    remap_kernel(peers, bands, refs[:10], *refs[10:])


def remap_kernel(
    peers,
    bands,
    sources,
    new_column,
    partial,
    wave,
    fixed,
    column,
    fast_state,
    depth,
    wet_mask,
    surface,
    coupling,
    emission,
    weights,
    send_block,
    link_slot,
    mine,
    got,
    table,
    wide,
    turned,
    linked,
    forcing,
    field_a,
    field_e,
    field_w,
    edge_e,
    edge_w,
    push_a,
    push_e,
    push_w,
    pedge_e,
    pedge_w,
    loaded,
    block_send,
    block_recv,
    field_send,
    field_recv,
    push_send,
    push_recv,
):
    comp = lax.axis_index("comp")
    row = lax.axis_index("row")
    col = lax.axis_index("col")
    slots = send_block.shape[1]
    head = table_rows(peers)
    bits = peers.bit_length() - 1
    up_ok = row < bands - 1
    down_ok = row > 0

    def at(dr, dc):
        return {"row": row + dr, "col": lax.rem(col + dc + peers, peers)}

    def reaches(dr):
        return up_ok if dr > 0 else down_ok

    def guarded(dr, act):
        if dr == 0:
            act()
        else:
            pl.when(reaches(dr))(act)

    held = (
        column,
        fast_state,
        depth,
        wet_mask,
        surface,
        coupling,
        emission,
        weights,
        send_block,
        link_slot,
    )

    def load(i):
        return pltpu.make_async_copy(sources[i], held[i], loaded.at[i])

    for i in (4, 3, 8, 1, 2, 7, 9, 5, 0, 6):
        load(i).start()

    barrier = pltpu.get_barrier_semaphore()

    def greet(device):
        pl.semaphore_signal(barrier, inc=1, device_id=device, device_id_type=MESH)

    greet({"comp": 1 - comp})
    for b in range(bits):
        greet({"col": col ^ (1 << b)})
    for dr, dc in TURNS:
        guarded(dr, functools.partial(greet, at(dr, dc)))

    for i in (8, 3, 4):
        load(i).wait()
    wet = wet_mask[...].astype(jnp.float32)
    table[...] = jnp.zeros_like(table)
    table[0:peers, 0:slots] = send_block[...].astype(jnp.float32)
    mine[0:head] = table[...].astype(jnp.bfloat16)
    for q in range(Q):
        mine[head + q * H : head + (q + 1) * H] = (surface[q] * wet).astype(jnp.bfloat16)

    beyond = up_ok.astype(jnp.int32) + down_ok.astype(jnp.int32)
    pl.semaphore_wait(barrier, 1 + bits + 2 + 3 * beyond)

    chunk_rows = Q * H // CHUNKS

    def span_of(chunk):
        if chunk == 0:
            return pl.ds(0, head + chunk_rows)
        return pl.ds(head + chunk * chunk_rows, chunk_rows)

    def block_copy(mask, bit, chunk):
        source = col ^ mask
        index = (mask | bit) * CHUNKS + chunk
        return pltpu.make_async_remote_copy(
            src_ref=got.at[source, span_of(chunk)],
            dst_ref=got.at[source, span_of(chunk)],
            send_sem=block_send.at[index],
            recv_sem=block_recv.at[index],
            device_id={"col": col ^ bit},
            device_id_type=MESH,
        )

    def arrival(mask, chunk):
        source = col ^ mask
        index = mask * CHUNKS + chunk
        if mask == 0:
            return pltpu.make_async_remote_copy(
                src_ref=mine.at[span_of(chunk)],
                dst_ref=got.at[col, span_of(chunk)],
                send_sem=block_send.at[index],
                recv_sem=block_recv.at[index],
                device_id={"comp": 1 - comp},
                device_id_type=MESH,
            )
        bit = mask & -mask
        return pltpu.make_async_remote_copy(
            src_ref=got.at[source, span_of(chunk)],
            dst_ref=got.at[source, span_of(chunk)],
            send_sem=block_send.at[index],
            recv_sem=block_recv.at[index],
            device_id={"col": col ^ bit},
            device_id_type=MESH,
        )

    def halo_copy(dr, dc, middle, east, west, land_e, land_w, send, recv):
        index = TURNS.index((dr, dc))
        land = pl.ds(H - H * dr, H)
        if dc == 0:
            src, dst = middle.at[:, pl.ds(H, H)], middle.at[:, land]
        elif dc > 0:
            src, dst = east, land_w.at[:, land]
        else:
            src, dst = west, land_e.at[:, land]
        return pltpu.make_async_remote_copy(
            src_ref=src,
            dst_ref=dst,
            send_sem=send.at[index],
            recv_sem=recv.at[index],
            device_id=at(dr, dc),
            device_id_type=MESH,
        )

    field_halo = (field_a, edge_e, edge_w, field_e, field_w, field_send, field_recv)
    push_halo = (push_a, pedge_e, pedge_w, push_e, push_w, push_send, push_recv)

    def send_halo(halo):
        for dr, dc in TURNS:
            guarded(dr, lambda dr=dr, dc=dc: halo_copy(dr, dc, *halo).start())

    def await_halo(halo):
        for dr, dc in TURNS:
            guarded(-dr, lambda dr=dr, dc=dc: halo_copy(dr, dc, *halo).wait_recv())

    def drain_halo(halo):
        for dr, dc in TURNS:
            guarded(dr, lambda dr=dr, dc=dc: halo_copy(dr, dc, *halo).wait_send())

    for chunk in range(CHUNKS):
        arrival(0, chunk).start()

    lane = lax.broadcasted_iota(jnp.int32, (H, W), 1)

    def pack(fields, east, west, tile):
        low = jnp.zeros((H, W), jnp.float32)
        high = jnp.zeros((H, W), jnp.float32)
        for i, cells in enumerate(fields):
            here = (lane >= i * PART) & (lane < (i + 1) * PART)
            first = cells if i == 0 else pltpu.roll(cells, i * PART, 1)
            turn = (i * PART - (W - PART)) % W
            last = cells if turn == 0 else pltpu.roll(cells, turn, 1)
            low = jnp.where(here, first, low)
            high = jnp.where(here, last, high)
        west[tile] = low
        east[tile] = high

    own = slice(H, 2 * H)
    for i in (1, 2):
        load(i).wait()
    statics = [fast_state[i] for i in range(FAST)] + [depth[...], wet]
    for i, cells in enumerate(statics):
        field_a[i, own] = cells
    pack(statics[:4], edge_e, edge_w, 0)
    pack(statics[4:], edge_e, edge_w, 1)

    @pl.when(jnp.logical_not(down_ok))
    def _():
        for ref in (field_a, field_e, field_w, push_a, push_e, push_w):
            ref[:, 0:H] = jnp.zeros_like(ref[:, 0:H])

    @pl.when(jnp.logical_not(up_ok))
    def _():
        for ref in (field_a, field_e, field_w, push_a, push_e, push_w):
            ref[:, 2 * H : 3 * H] = jnp.zeros_like(ref[:, 2 * H : 3 * H])

    send_halo(field_halo)

    load(7).wait()
    wide[...] = weights[...].astype(jnp.float32)
    for k in range(K):
        for d in range(SPAN):
            plane = wide[pl.ds(k * SPAN + d, H, stride=K * SPAN), :]
            turn = (d - SPAN // 2) % W
            turned[k * SPAN + d] = plane if turn == 0 else pltpu.roll(plane, turn, 1)

    links = H * K
    rows_l = lax.broadcasted_iota(jnp.int32, (links, links), 0)
    lanes_l = lax.broadcasted_iota(jnp.int32, (links, links), 1)

    def hot(condition):
        return jnp.where(condition, 1.0, 0.0).astype(jnp.bfloat16)

    def dot_nt(a, b):
        return lax.dot_general(
            a, b, (((1,), (1,)), ((), ())), preferred_element_type=jnp.float32
        )

    load(9).wait()
    order = hot(lanes_l == (rows_l & (H - 1)) * K + (rows_l >> 5))
    by_slot = hot(rows_l == link_slot[...])
    slot_of_link = dot_nt(order, by_slot).astype(jnp.bfloat16)

    waited = []
    order_of = mask_order(peers)
    senders = [m for m in order_of if m == 0 or lower_bits(m, peers)]
    leaves = [m for m in order_of if m not in senders]

    def receive(mask, chunk):
        arrival(mask, chunk).wait_recv()
        for bit in lower_bits(mask, peers):
            block_copy(mask, bit, chunk).start()

    for mask in senders:
        for chunk in range(CHUNKS):
            receive(mask, chunk)
    pick = None
    per_chunk = Q // CHUNKS
    for chunk in range(CHUNKS):
        for mask in leaves:
            receive(mask, chunk)
        if chunk == 0:
            pieces = []
            rows_h = lax.broadcasted_iota(jnp.int32, (H, W), 0)
            rows_t = lax.broadcasted_iota(jnp.int32, (head, W), 0)
            for s in range(peers):
                listed = got[s, 0:head].astype(jnp.float32)
                chosen = jnp.sum(jnp.where(rows_t == col, listed, 0.0), axis=0, keepdims=True)
                chosen = jnp.broadcast_to(chosen, (H, W)).astype(jnp.int32)
                turn = s * slots % W
                chosen = chosen if turn == 0 else pltpu.roll(chosen, turn, 1)
                here = (lane >= s * slots) & (lane < (s + 1) * slots)
                pieces.append(hot(here & (chosen == rows_h)))
            block_of_slot = jnp.concatenate(pieces, axis=0)
            pick = dot_nt(slot_of_link, block_of_slot).astype(jnp.bfloat16)
        for pair in range(per_chunk // 2):
            first = chunk * per_chunk + 2 * pair
            cells = []
            for q in (first, first + 1):
                tall = got[:, head + q * H : head + (q + 1) * H, :]
                cells.append(tall.reshape(peers * H, W))
            linked[...] = jnp.dot(
                pick, jnp.concatenate(cells, axis=1), preferred_element_type=jnp.float32
            )
            for side in range(2):
                total = jnp.zeros((H, W), jnp.float32)
                for d in range(SPAN):
                    part = jnp.zeros((H, W), jnp.float32)
                    for k in range(K):
                        part = part + (
                            linked[k * H : (k + 1) * H, side * W : (side + 1) * W]
                            * turned[k * SPAN + d]
                        )
                    turn = (SPAN // 2 - d) % W
                    total = total + (part if turn == 0 else pltpu.roll(part, turn, 1))
                forcing[first + side] = total

    load(5).wait()

    def driven(m, rows):
        total = coupling[0, m] * forcing[0, rows]
        for q in range(1, Q):
            total = total + coupling[q, m] * forcing[q, rows]
        return total

    everywhere = slice(0, H)
    pushes = [driven(L + i, everywhere) * (1.0 / SUBSTEPS) for i in range(FAST)]
    for i in range(FAST):
        push_a[i, own] = pushes[i]
    pack(pushes, pedge_e, pedge_w, 0)
    send_halo(push_halo)

    for i in (0, 6):
        load(i).wait()
    for m in range(L):
        new_column[m] = column[m] + driven(m, everywhere)
    for q in range(Q):
        total = emission[q, 0] * new_column[0]
        for m in range(1, L):
            total = total + emission[q, m] * new_column[m]
        partial[q] = total
    await_halo(field_halo)

    lane_r = lax.broadcasted_iota(jnp.int32, (ROWS, W), 1)

    def beside(east, west, i):
        tile, place = divmod(i, W // PART)
        near = east[tile]
        near = near if place == 0 else pltpu.roll(near, (W - place * PART) % W, 1)
        turn = (W - PART - place * PART) % W
        far = west[tile]
        far = far if turn == 0 else pltpu.roll(far, turn, 1)
        cells = jnp.where(lane_r < PART, near, 0.0)
        return jnp.where(lane_r >= W - PART, far, cells)

    scale = [STEP_SIZE, 1.0, 1.0, STEP_SIZE * STEP_SIZE, 1.0]
    for i in range(5):
        ref = wave.at[i] if i < FAST else fixed.at[i - FAST]
        ref[0] = field_a[i] * scale[i]
        ref[1] = beside(field_e, field_w, i) * scale[i]
    await_halo(push_halo)
    pscale = [STEP_SIZE, 1.0, 1.0]
    for i in range(FAST):
        fixed[2 + i, 0] = push_a[i] * pscale[i]
        fixed[2 + i, 1] = beside(push_e, push_w, i) * pscale[i]

    for chunk in range(CHUNKS):
        for mask in range(peers):
            arrival(mask, chunk).wait_send()
    drain_halo(field_halo)
    drain_halo(push_halo)


def wave_kernel(
    bands,
    new_column,
    partial,
    start,
    fixed,
    emission_source,
    column_out,
    final_out,
    surface_out,
    wave,
    totals,
    fast_final,
    next_surface,
    emission,
    sems,
):
    own = slice(H, 2 * H)
    up_ok = lax.axis_index("row") < bands - 1
    load = pltpu.make_async_copy(emission_source, emission, sems.at[0])
    load.start()
    column_copy = pltpu.make_async_copy(new_column, column_out, sems.at[1])
    column_copy.start()
    wave[...] = start[...]
    totals[...] = jnp.zeros_like(totals)
    lane8 = lax.broadcasted_iota(jnp.int32, (8, W), 1)
    sub8 = lax.broadcasted_iota(jnp.int32, (8, W), 0)
    west_rim = lane8 == 0
    east_rim = lane8 == W - 1
    south_rim = sub8 == 0
    north_rim = sub8 == 7
    top = jnp.where(up_ok, 1.0, 0.0).astype(jnp.float32)

    def sweep(low, high):
        south_prev = [jnp.zeros((8, W), jnp.float32)] * 2
        held = None
        for block in range(low, high + 2):
            rows = slice(8 * block, 8 * block + 8)
            now = None
            if block <= high:
                flow_e = [wave[1, t, rows] for t in range(2)]
                flow_n = [wave[2, t, rows] for t in range(2)]
                deep = [fixed[0, t, rows] for t in range(2)]
                flux_e = [deep[t] * flow_e[t] for t in range(2)]
                flux_n = [deep[t] * flow_n[t] for t in range(2)]
                spun = [pltpu.roll(flux_e[t], 1, 0 + 1) for t in range(2)]
                lifted = [pltpu.roll(flux_n[t], 1, 0) for t in range(2)]
                high_new = []
                for t in range(2):
                    from_west = jnp.where(west_rim, spun[1 - t], spun[t])
                    from_south = jnp.where(south_rim, south_prev[t], lifted[t])
                    level = (
                        wave[0, t, rows]
                        - ((flux_e[t] - from_west) + (flux_n[t] - from_south))
                        + fixed[2, t, rows]
                    )
                    if block == 2 * H // 8:
                        level = level * top
                    wave[0, t, rows] = level
                    high_new.append(level)
                if 4 <= block < 8:
                    orows = slice(8 * block - H, 8 * block - H + 8)
                    totals[0, orows] += high_new[0]
                south_prev = lifted
                down = [pltpu.roll(high_new[t], 7, 0) for t in range(2)]
                now = (rows, block, high_new, flow_e, flow_n, down)
            if held is not None:
                rows, block_h, level, flow_e, flow_n, down = held
                spun = [pltpu.roll(level[t], W - 1, 1) for t in range(2)]
                for t in range(2):
                    to_east = jnp.where(east_rim, spun[1 - t], spun[t])
                    if now is None:
                        to_north = down[t]
                    else:
                        to_north = jnp.where(north_rim, now[5][t], down[t])
                    open_cells = fixed[1, t, rows]
                    east = open_cells * (
                        DAMPING * flow_e[t] - (to_east - level[t]) + fixed[3, t, rows]
                    )
                    north = open_cells * (
                        DAMPING * flow_n[t] - (to_north - level[t]) + fixed[4, t, rows]
                    )
                    wave[1, t, rows] = east
                    wave[2, t, rows] = north
                    if t == 0 and 4 <= block_h < 8:
                        orows = slice(8 * block_h - H, 8 * block_h - H + 8)
                        totals[1, orows] += east
                        totals[2, orows] += north
            held = now

    for group in range(SUBSTEPS // 8):

        def step(_, carry, group=group):
            sweep(group, ROWS // 8 - 1 - group)
            return carry

        lax.fori_loop(0, 8, step, 0)

    back = [1.0 / STEP_SIZE, 1.0, 1.0]
    for i in range(FAST):
        fast_final[i] = wave[i, 0, own] * back[i]
    final_copy = pltpu.make_async_copy(fast_final, final_out, sems.at[2])
    final_copy.start()
    load.wait()
    mean = [totals[i] * (back[i] / SUBSTEPS) for i in range(FAST)]
    for q in range(Q):
        total = partial[q]
        for i in range(FAST):
            total = total + emission[q, L + i] * mean[i]
        next_surface[q] = jnp.tanh(total)
    surface_copy = pltpu.make_async_copy(next_surface, surface_out, sems.at[3])
    surface_copy.start()
    surface_copy.wait()
    final_copy.wait()
    column_copy.wait()


def solution(mesh):
    peers = mesh.shape["col"]
    bands = mesh.shape["row"]
    head = table_rows(peers)

    def body(
        column,
        fast_state,
        wave_depth,
        wet_mask,
        surface,
        coupling,
        emission,
        remap_weight,
        send_block,
        link_slot,
    ):
        f32 = jnp.float32
        vmem = pl.BlockSpec(memory_space=pltpu.VMEM)
        hbm = pl.BlockSpec(memory_space=pltpu.HBM)
        dma = pltpu.SemaphoreType.DMA
        small_emission = emission[0]
        mid = pl.pallas_call(
            functools.partial(kernel, peers, bands),
            out_shape=(
                pltpu.VMEM((L, H, W), f32),
                pltpu.VMEM((Q, H, W), f32),
                pltpu.VMEM((FAST, 2, ROWS, W), f32),
                pltpu.VMEM((5, 2, ROWS, W), f32),
            ),
            in_specs=[hbm] * 10,
            out_specs=(vmem,) * 4,
            scratch_shapes=[
                pltpu.VMEM((L, H, W), f32),
                pltpu.VMEM((FAST, H, W), f32),
                pltpu.VMEM((H, W), f32),
                pltpu.VMEM((H, W), jnp.int32),
                pltpu.VMEM((Q, H, W), f32),
                pltpu.SMEM(coupling.shape[:0:-1], f32),
                pltpu.SMEM(emission.shape[1:], f32),
                pltpu.VMEM((H * K * SPAN, W), jnp.bfloat16),
                pltpu.VMEM(send_block.shape[2:], jnp.int32),
                pltpu.VMEM(link_slot.shape[1:], jnp.int32),
                pltpu.VMEM((head + Q * H, W), jnp.bfloat16),
                pltpu.VMEM((peers, head + Q * H, W), jnp.bfloat16),
                pltpu.VMEM((head, W), f32),
                pltpu.VMEM((H * K * SPAN, W), f32),
                pltpu.VMEM((K * SPAN, H, W), f32),
                pltpu.VMEM((H * K, 2 * W), f32),
                pltpu.VMEM((Q, H, W), f32),
                pltpu.VMEM((5, ROWS, W), f32),
                pltpu.VMEM((2, ROWS, W), f32),
                pltpu.VMEM((2, ROWS, W), f32),
                pltpu.VMEM((2, H, W), f32),
                pltpu.VMEM((2, H, W), f32),
                pltpu.VMEM((FAST, ROWS, W), f32),
                pltpu.VMEM((1, ROWS, W), f32),
                pltpu.VMEM((1, ROWS, W), f32),
                pltpu.VMEM((1, H, W), f32),
                pltpu.VMEM((1, H, W), f32),
                dma((10,)),
                dma((peers * CHUNKS,)),
                dma((peers * CHUNKS,)),
                dma((8,)),
                dma((8,)),
                dma((8,)),
                dma((8,)),
            ],
            compiler_params=pltpu.CompilerParams(
                collective_id=0, has_side_effects=True, vmem_limit_bytes=40 << 20
            ),
        )(
*[pltpu.with_memory_space_constraint(x, pltpu.HBM) for x in (column[0],
            fast_state[0],
            wave_depth[0],
            wet_mask[0],
            surface[0],
            coupling[0].T,
            small_emission,
            remap_weight.reshape(H * K * SPAN, W),
            send_block[0, 0],
            link_slot[0],)]
        )
        outs = pl.pallas_call(
            functools.partial(wave_kernel, bands),
            out_shape=(
                jax.ShapeDtypeStruct((L, H, W), f32),
                jax.ShapeDtypeStruct((FAST, H, W), f32),
                jax.ShapeDtypeStruct((Q, H, W), f32),
            ),
            in_specs=[vmem] * 4 + [hbm],
            out_specs=(hbm,) * 3,
            scratch_shapes=[
                pltpu.VMEM((FAST, 2, ROWS, W), f32),
                pltpu.VMEM((FAST, H, W), f32),
                pltpu.VMEM((FAST, H, W), f32),
                pltpu.VMEM((Q, H, W), f32),
                pltpu.SMEM(emission.shape[1:], f32),
                dma((4,)),
            ],
            compiler_params=pltpu.CompilerParams(vmem_limit_bytes=16 << 20),
        )(*mid, small_emission)
        return tuple(out[None] for out in outs)

    placed = (
        P("comp", None, "row", "col"),
        P("comp", None, "row", "col"),
        P("comp", "row", "col"),
        P("comp", "row", "col"),
        P("comp", None, "row", "col"),
        P("comp", None, None),
        P("comp", None, None),
        P("comp", "row", "col", None, None),
        P("comp", "row", "col", None),
        P("comp", "row", "col"),
    )
    return jax.shard_map(
        body,
        mesh=mesh,
        in_specs=placed,
        out_specs=(
            P("comp", None, "row", "col"),
            P("comp", None, "row", "col"),
            P("comp", None, "row", "col"),
        ),
        check_vma=False,
    )
```

```python
import functools

import jax
import jax.numpy as jnp
from jax import lax
from jax.experimental import pallas as pl
from jax.experimental.pallas import tpu as pltpu
from jax.sharding import PartitionSpec as P

H = 32
W = 128
K = 4
SPAN = 4
Q = 8
L = 8
SUBSTEPS = 32
FAST = 3
STEP_SIZE = 0.35
DAMPING = 0.97
CHUNKS = 2
PART = 32
ROWS = 3 * H
MESH = pl.DeviceIdType.MESH
TURNS = [(dr, dc) for dr in (-1, 0, 1) for dc in (-1, 0, 1) if (dr, dc) != (0, 0)]


def table_rows(peers):
    return max(16, -(-peers // 16) * 16)


def mask_order(peers):
    bits = peers.bit_length() - 1
    return sorted(range(peers), key=lambda m: int(format(m, "b").zfill(bits)[::-1], 2))


def lower_bits(mask, peers):
    bits = [1 << b for b in reversed(range(peers.bit_length() - 1))]
    return [b for b in bits if mask == 0 or b < (mask & -mask)]


def kernel(peers, bands, *refs):
    remap_kernel(peers, bands, refs[:10], *refs[10:])


def remap_kernel(
    peers,
    bands,
    sources,
    new_column,
    partial,
    wave,
    fixed,
    column,
    fast_state,
    depth,
    wet_mask,
    surface,
    coupling,
    emission,
    weights,
    send_block,
    link_slot,
    mine,
    got,
    table,
    wide,
    turned,
    linked,
    forcing,
    field_a,
    field_e,
    field_w,
    edge_e,
    edge_w,
    push_a,
    push_e,
    push_w,
    pedge_e,
    pedge_w,
    loaded,
    block_send,
    block_recv,
    field_send,
    field_recv,
    push_send,
    push_recv,
):
    comp = lax.axis_index("comp")
    row = lax.axis_index("row")
    col = lax.axis_index("col")
    slots = send_block.shape[1]
    head = table_rows(peers)
    bits = peers.bit_length() - 1
    up_ok = row < bands - 1
    down_ok = row > 0

    def at(dr, dc):
        return {"row": row + dr, "col": lax.rem(col + dc + peers, peers)}

    def reaches(dr):
        return up_ok if dr > 0 else down_ok

    def guarded(dr, act):
        if dr == 0:
            act()
        else:
            pl.when(reaches(dr))(act)

    held = (
        column,
        fast_state,
        depth,
        wet_mask,
        surface,
        coupling,
        emission,
        weights,
        send_block,
        link_slot,
    )

    def load(i):
        return pltpu.make_async_copy(sources[i], held[i], loaded.at[i])

    for i in (4, 3, 8, 1, 2, 7, 9, 5, 0, 6):
        load(i).start()

    barrier = pltpu.get_barrier_semaphore()

    def greet(device):
        pl.semaphore_signal(barrier, inc=1, device_id=device, device_id_type=MESH)

    greet({"comp": 1 - comp})
    for b in range(bits):
        greet({"col": col ^ (1 << b)})
    for dr, dc in TURNS:
        guarded(dr, functools.partial(greet, at(dr, dc)))

    for i in (8, 3, 4):
        load(i).wait()
    wet = wet_mask[...].astype(jnp.float32)
    table[...] = jnp.zeros_like(table)
    table[0:peers, 0:slots] = send_block[...].astype(jnp.float32)
    mine[0:head] = table[...].astype(jnp.bfloat16)
    for q in range(Q):
        mine[head + q * H : head + (q + 1) * H] = (surface[q] * wet).astype(jnp.bfloat16)

    beyond = up_ok.astype(jnp.int32) + down_ok.astype(jnp.int32)
    pl.semaphore_wait(barrier, 1 + bits + 2 + 3 * beyond)

    chunk_rows = Q * H // CHUNKS

    def span_of(chunk):
        if chunk == 0:
            return pl.ds(0, head + chunk_rows)
        return pl.ds(head + chunk * chunk_rows, chunk_rows)

    def block_copy(mask, bit, chunk):
        source = col ^ mask
        index = (mask | bit) * CHUNKS + chunk
        return pltpu.make_async_remote_copy(
            src_ref=got.at[source, span_of(chunk)],
            dst_ref=got.at[source, span_of(chunk)],
            send_sem=block_send.at[index],
            recv_sem=block_recv.at[index],
            device_id={"col": col ^ bit},
            device_id_type=MESH,
        )

    def arrival(mask, chunk):
        source = col ^ mask
        index = mask * CHUNKS + chunk
        if mask == 0:
            return pltpu.make_async_remote_copy(
                src_ref=mine.at[span_of(chunk)],
                dst_ref=got.at[col, span_of(chunk)],
                send_sem=block_send.at[index],
                recv_sem=block_recv.at[index],
                device_id={"comp": 1 - comp},
                device_id_type=MESH,
            )
        bit = mask & -mask
        return pltpu.make_async_remote_copy(
            src_ref=got.at[source, span_of(chunk)],
            dst_ref=got.at[source, span_of(chunk)],
            send_sem=block_send.at[index],
            recv_sem=block_recv.at[index],
            device_id={"col": col ^ bit},
            device_id_type=MESH,
        )

    def halo_copy(dr, dc, middle, east, west, land_e, land_w, send, recv):
        index = TURNS.index((dr, dc))
        land = pl.ds(H - H * dr, H)
        if dc == 0:
            src, dst = middle.at[:, pl.ds(H, H)], middle.at[:, land]
        elif dc > 0:
            src, dst = east, land_w.at[:, land]
        else:
            src, dst = west, land_e.at[:, land]
        return pltpu.make_async_remote_copy(
            src_ref=src,
            dst_ref=dst,
            send_sem=send.at[index],
            recv_sem=recv.at[index],
            device_id=at(dr, dc),
            device_id_type=MESH,
        )

    field_halo = (field_a, edge_e, edge_w, field_e, field_w, field_send, field_recv)
    push_halo = (push_a, pedge_e, pedge_w, push_e, push_w, push_send, push_recv)

    def send_halo(halo):
        for dr, dc in TURNS:
            guarded(dr, lambda dr=dr, dc=dc: halo_copy(dr, dc, *halo).start())

    def await_halo(halo):
        for dr, dc in TURNS:
            guarded(-dr, lambda dr=dr, dc=dc: halo_copy(dr, dc, *halo).wait_recv())

    def drain_halo(halo):
        for dr, dc in TURNS:
            guarded(dr, lambda dr=dr, dc=dc: halo_copy(dr, dc, *halo).wait_send())

    for chunk in range(CHUNKS):
        arrival(0, chunk).start()

    lane = lax.broadcasted_iota(jnp.int32, (H, W), 1)

    def pack(fields, east, west, tile):
        low = jnp.zeros((H, W), jnp.float32)
        high = jnp.zeros((H, W), jnp.float32)
        for i, cells in enumerate(fields):
            here = (lane >= i * PART) & (lane < (i + 1) * PART)
            first = cells if i == 0 else pltpu.roll(cells, i * PART, 1)
            turn = (i * PART - (W - PART)) % W
            last = cells if turn == 0 else pltpu.roll(cells, turn, 1)
            low = jnp.where(here, first, low)
            high = jnp.where(here, last, high)
        west[tile] = low.astype(jnp.bfloat16)
        east[tile] = high.astype(jnp.bfloat16)

    own = slice(H, 2 * H)
    for i in (1, 2):
        load(i).wait()
    statics = [fast_state[i] for i in range(FAST)] + [depth[...], wet]
    for i, cells in enumerate(statics):
        field_a[i, own] = cells.astype(jnp.bfloat16)
    pack(statics[:4], edge_e, edge_w, 0)
    pack(statics[4:], edge_e, edge_w, 1)

    @pl.when(jnp.logical_not(down_ok))
    def _():
        for ref in (field_a, field_e, field_w, push_a, push_e, push_w):
            ref[:, 0:H] = jnp.zeros_like(ref[:, 0:H])

    @pl.when(jnp.logical_not(up_ok))
    def _():
        for ref in (field_a, field_e, field_w, push_a, push_e, push_w):
            ref[:, 2 * H : 3 * H] = jnp.zeros_like(ref[:, 2 * H : 3 * H])

    send_halo(field_halo)

    load(7).wait()
    wide[...] = weights[...].astype(jnp.float32)
    for k in range(K):
        for d in range(SPAN):
            plane = wide[pl.ds(k * SPAN + d, H, stride=K * SPAN), :]
            turn = (d - SPAN // 2) % W
            turned[k * SPAN + d] = plane if turn == 0 else pltpu.roll(plane, turn, 1)

    links = H * K
    rows_l = lax.broadcasted_iota(jnp.int32, (links, links), 0)
    lanes_l = lax.broadcasted_iota(jnp.int32, (links, links), 1)

    def hot(condition):
        return jnp.where(condition, 1.0, 0.0).astype(jnp.bfloat16)

    def dot_nt(a, b):
        return lax.dot_general(
            a, b, (((1,), (1,)), ((), ())), preferred_element_type=jnp.float32
        )

    load(9).wait()
    order = hot(lanes_l == (rows_l & (H - 1)) * K + (rows_l >> 5))
    by_slot = hot(rows_l == link_slot[...])
    slot_of_link = dot_nt(order, by_slot).astype(jnp.bfloat16)

    waited = []
    order_of = mask_order(peers)
    senders = [m for m in order_of if m == 0 or lower_bits(m, peers)]
    leaves = [m for m in order_of if m not in senders]

    def receive(mask, chunk):
        arrival(mask, chunk).wait_recv()
        for bit in lower_bits(mask, peers):
            block_copy(mask, bit, chunk).start()

    for mask in senders:
        for chunk in range(CHUNKS):
            receive(mask, chunk)
    pick = None
    per_chunk = Q // CHUNKS
    for chunk in range(CHUNKS):
        for mask in leaves:
            receive(mask, chunk)
        if chunk == 0:
            pieces = []
            rows_h = lax.broadcasted_iota(jnp.int32, (H, W), 0)
            rows_t = lax.broadcasted_iota(jnp.int32, (head, W), 0)
            for s in range(peers):
                listed = got[s, 0:head].astype(jnp.float32)
                chosen = jnp.sum(jnp.where(rows_t == col, listed, 0.0), axis=0, keepdims=True)
                chosen = jnp.broadcast_to(chosen, (H, W)).astype(jnp.int32)
                turn = s * slots % W
                chosen = chosen if turn == 0 else pltpu.roll(chosen, turn, 1)
                here = (lane >= s * slots) & (lane < (s + 1) * slots)
                pieces.append(hot(here & (chosen == rows_h)))
            block_of_slot = jnp.concatenate(pieces, axis=0)
            pick = dot_nt(slot_of_link, block_of_slot).astype(jnp.bfloat16)
        for pair in range(per_chunk // 2):
            first = chunk * per_chunk + 2 * pair
            cells = []
            for q in (first, first + 1):
                tall = got[:, head + q * H : head + (q + 1) * H, :]
                cells.append(tall.reshape(peers * H, W))
            linked[...] = jnp.dot(
                pick, jnp.concatenate(cells, axis=1), preferred_element_type=jnp.float32
            )
            for side in range(2):
                total = jnp.zeros((H, W), jnp.float32)
                for d in range(SPAN):
                    part = jnp.zeros((H, W), jnp.float32)
                    for k in range(K):
                        part = part + (
                            linked[k * H : (k + 1) * H, side * W : (side + 1) * W]
                            * turned[k * SPAN + d]
                        )
                    turn = (SPAN // 2 - d) % W
                    total = total + (part if turn == 0 else pltpu.roll(part, turn, 1))
                forcing[first + side] = total

    load(5).wait()

    def driven(m, rows):
        total = coupling[0, m] * forcing[0, rows]
        for q in range(1, Q):
            total = total + coupling[q, m] * forcing[q, rows]
        return total

    everywhere = slice(0, H)
    pushes = [driven(L + i, everywhere) * (1.0 / SUBSTEPS) for i in range(FAST)]
    for i in range(FAST):
        push_a[i, own] = pushes[i].astype(jnp.bfloat16)
    pack(pushes, pedge_e, pedge_w, 0)
    send_halo(push_halo)

    for i in (0, 6):
        load(i).wait()
    for m in range(L):
        new_column[m] = column[m] + driven(m, everywhere)
    for q in range(Q):
        total = emission[q, 0] * new_column[0]
        for m in range(1, L):
            total = total + emission[q, m] * new_column[m]
        partial[q] = total
    await_halo(field_halo)

    lane_r = lax.broadcasted_iota(jnp.int32, (ROWS, W), 1)

    def beside(east, west, i):
        tile, place = divmod(i, W // PART)
        near = east[tile].astype(jnp.float32)
        near = near if place == 0 else pltpu.roll(near, (W - place * PART) % W, 1)
        turn = (W - PART - place * PART) % W
        far = west[tile].astype(jnp.float32)
        far = far if turn == 0 else pltpu.roll(far, turn, 1)
        cells = jnp.where(lane_r < PART, near, 0.0)
        return jnp.where(lane_r >= W - PART, far, cells)

    scale = [STEP_SIZE, 1.0, 1.0, STEP_SIZE * STEP_SIZE, 1.0]
    for i in range(5):
        ref = wave.at[i] if i < FAST else fixed.at[i - FAST]
        for rows in (slice(0, H), slice(2 * H, ROWS)):
            ref[0, rows] = field_a[i, rows].astype(jnp.float32) * scale[i]
        ref[0, own] = statics[i] * scale[i]
        ref[1] = beside(field_e, field_w, i) * scale[i]
    await_halo(push_halo)
    pscale = [STEP_SIZE, 1.0, 1.0]
    for i in range(FAST):
        for rows in (slice(0, H), slice(2 * H, ROWS)):
            fixed[2 + i, 0, rows] = push_a[i, rows].astype(jnp.float32) * pscale[i]
        fixed[2 + i, 0, own] = pushes[i] * pscale[i]
        fixed[2 + i, 1] = beside(push_e, push_w, i) * pscale[i]

    for chunk in range(CHUNKS):
        for mask in range(peers):
            arrival(mask, chunk).wait_send()
    drain_halo(field_halo)
    drain_halo(push_halo)


def wave_kernel(
    bands,
    new_column,
    partial,
    start,
    fixed,
    emission_source,
    column_out,
    final_out,
    surface_out,
    even,
    odd,
    fast_final,
    next_surface,
    emission,
    sems,
):
    own = slice(H, 2 * H)
    up_ok = lax.axis_index("row") < bands - 1
    load = pltpu.make_async_copy(emission_source, emission, sems.at[0])
    load.start()
    column_copy = pltpu.make_async_copy(new_column, column_out, sems.at[1])
    column_copy.start()
    even[...] = start[...]
    lane8 = lax.broadcasted_iota(jnp.int32, (8, W), 1)
    sub8 = lax.broadcasted_iota(jnp.int32, (8, W), 0)
    west_rim = lane8 == 0
    east_rim = lane8 == W - 1
    south_rim = sub8 == 0
    north_rim = sub8 == 7
    top = jnp.where(up_ok, 1.0, 0.0).astype(jnp.float32)

    def sweep(wave, after, totals, low, high):
        totals = list(totals)
        south_prev = [jnp.zeros((8, W), jnp.float32)] * 2
        held = None
        for block in range(low, high + 2):
            rows = slice(8 * block, 8 * block + 8)
            now = None
            if block <= high:
                flow_e = [wave[1, t, rows] for t in range(2)]
                flow_n = [wave[2, t, rows] for t in range(2)]
                deep = [fixed[0, t, rows] for t in range(2)]
                flux_e = [deep[t] * flow_e[t] for t in range(2)]
                flux_n = [deep[t] * flow_n[t] for t in range(2)]
                spun = [pltpu.roll(flux_e[t], 1, 0 + 1) for t in range(2)]
                lifted = [pltpu.roll(flux_n[t], 1, 0) for t in range(2)]
                high_new = []
                for t in range(2):
                    from_west = jnp.where(west_rim, spun[1 - t], spun[t])
                    from_south = jnp.where(south_rim, south_prev[t], lifted[t])
                    level = (
                        wave[0, t, rows]
                        - ((flux_e[t] - from_west) + (flux_n[t] - from_south))
                        + fixed[2, t, rows]
                    )
                    if block == 2 * H // 8:
                        level = level * top
                    after[0, t, rows] = level
                    high_new.append(level)
                if 4 <= block < 8:
                    totals[block - 4] = totals[block - 4] + high_new[0]
                south_prev = lifted
                down = [pltpu.roll(high_new[t], 7, 0) for t in range(2)]
                now = (rows, block, high_new, flow_e, flow_n, down)
            if held is not None:
                rows, block_h, level, flow_e, flow_n, down = held
                spun = [pltpu.roll(level[t], W - 1, 1) for t in range(2)]
                for t in range(2):
                    to_east = jnp.where(east_rim, spun[1 - t], spun[t])
                    if now is None:
                        to_north = down[t]
                    else:
                        to_north = jnp.where(north_rim, now[5][t], down[t])
                    open_cells = fixed[1, t, rows]
                    east = open_cells * (
                        DAMPING * flow_e[t] - (to_east - level[t]) + fixed[3, t, rows]
                    )
                    north = open_cells * (
                        DAMPING * flow_n[t] - (to_north - level[t]) + fixed[4, t, rows]
                    )
                    after[1, t, rows] = east
                    after[2, t, rows] = north
                    if t == 0 and 4 <= block_h < 8:
                        totals[block_h] = totals[block_h] + east
                        totals[block_h + 4] = totals[block_h + 4] + north
            held = now
        return tuple(totals)

    sums = (jnp.zeros((8, W), jnp.float32),) * (FAST * H // 8)
    for group in range(SUBSTEPS // 8):

        def steps(_, sums, group=group):
            low, high = group, ROWS // 8 - 1 - group
            sums = sweep(even, odd, sums, low, high)
            return sweep(odd, even, sums, low, high)

        sums = lax.fori_loop(0, 4, steps, sums)
    totals = [jnp.concatenate(sums[4 * i : 4 * i + 4], axis=0) for i in range(FAST)]

    back = [1.0 / STEP_SIZE, 1.0, 1.0]
    for i in range(FAST):
        fast_final[i] = even[i, 0, own] * back[i]
    final_copy = pltpu.make_async_copy(fast_final, final_out, sems.at[2])
    final_copy.start()
    load.wait()
    mean = [totals[i] * (back[i] / SUBSTEPS) for i in range(FAST)]
    for q in range(Q):
        total = partial[q]
        for i in range(FAST):
            total = total + emission[q, L + i] * mean[i]
        next_surface[q] = jnp.tanh(total)
    surface_copy = pltpu.make_async_copy(next_surface, surface_out, sems.at[3])
    surface_copy.start()
    surface_copy.wait()
    final_copy.wait()
    column_copy.wait()


def solution(mesh):
    peers = mesh.shape["col"]
    bands = mesh.shape["row"]
    head = table_rows(peers)

    def body(
        column,
        fast_state,
        wave_depth,
        wet_mask,
        surface,
        coupling,
        emission,
        remap_weight,
        send_block,
        link_slot,
    ):
        f32 = jnp.float32
        vmem = pl.BlockSpec(memory_space=pltpu.VMEM)
        hbm = pl.BlockSpec(memory_space=pltpu.HBM)
        dma = pltpu.SemaphoreType.DMA
        small_emission = pltpu.with_memory_space_constraint(emission[0], pltpu.HBM)
        mid = pl.pallas_call(
            functools.partial(kernel, peers, bands),
            out_shape=(
                pltpu.VMEM((L, H, W), f32),
                pltpu.VMEM((Q, H, W), f32),
                pltpu.VMEM((FAST, 2, ROWS, W), f32),
                pltpu.VMEM((5, 2, ROWS, W), f32),
            ),
            in_specs=[hbm] * 10,
            out_specs=(vmem,) * 4,
            scratch_shapes=[
                pltpu.VMEM((L, H, W), f32),
                pltpu.VMEM((FAST, H, W), f32),
                pltpu.VMEM((H, W), f32),
                pltpu.VMEM((H, W), jnp.int32),
                pltpu.VMEM((Q, H, W), f32),
                pltpu.SMEM(coupling.shape[:0:-1], f32),
                pltpu.SMEM(emission.shape[1:], f32),
                pltpu.VMEM((H * K * SPAN, W), jnp.bfloat16),
                pltpu.VMEM(send_block.shape[2:], jnp.int32),
                pltpu.VMEM(link_slot.shape[1:], jnp.int32),
                pltpu.VMEM((head + Q * H, W), jnp.bfloat16),
                pltpu.VMEM((peers, head + Q * H, W), jnp.bfloat16),
                pltpu.VMEM((head, W), f32),
                pltpu.VMEM((H * K * SPAN, W), f32),
                pltpu.VMEM((K * SPAN, H, W), f32),
                pltpu.VMEM((H * K, 2 * W), f32),
                pltpu.VMEM((Q, H, W), f32),
                pltpu.VMEM((5, ROWS, W), jnp.bfloat16),
                pltpu.VMEM((2, ROWS, W), jnp.bfloat16),
                pltpu.VMEM((2, ROWS, W), jnp.bfloat16),
                pltpu.VMEM((2, H, W), jnp.bfloat16),
                pltpu.VMEM((2, H, W), jnp.bfloat16),
                pltpu.VMEM((FAST, ROWS, W), jnp.bfloat16),
                pltpu.VMEM((1, ROWS, W), jnp.bfloat16),
                pltpu.VMEM((1, ROWS, W), jnp.bfloat16),
                pltpu.VMEM((1, H, W), jnp.bfloat16),
                pltpu.VMEM((1, H, W), jnp.bfloat16),
                dma((10,)),
                dma((peers * CHUNKS,)),
                dma((peers * CHUNKS,)),
                dma((8,)),
                dma((8,)),
                dma((8,)),
                dma((8,)),
            ],
            compiler_params=pltpu.CompilerParams(
                collective_id=0, has_side_effects=True, vmem_limit_bytes=40 << 20
            ),
        )(
*[pltpu.with_memory_space_constraint(x, pltpu.HBM) for x in (column[0],
            fast_state[0],
            wave_depth[0],
            wet_mask[0],
            surface[0],
            coupling[0].T,
            small_emission,
            remap_weight.reshape(H * K * SPAN, W),
            send_block[0, 0],
            link_slot[0],)]
        )
        outs = pl.pallas_call(
            functools.partial(wave_kernel, bands),
            out_shape=(
                jax.ShapeDtypeStruct((L, H, W), f32),
                jax.ShapeDtypeStruct((FAST, H, W), f32),
                jax.ShapeDtypeStruct((Q, H, W), f32),
            ),
            in_specs=[vmem] * 4 + [hbm],
            out_specs=(hbm,) * 3,
            scratch_shapes=[
                pltpu.VMEM((FAST, 2, ROWS, W), f32),
                pltpu.VMEM((FAST, 2, ROWS, W), f32),
                pltpu.VMEM((FAST, H, W), f32),
                pltpu.VMEM((Q, H, W), f32),
                pltpu.SMEM(emission.shape[1:], f32),
                dma((4,)),
            ],
            compiler_params=pltpu.CompilerParams(vmem_limit_bytes=16 << 20),
        )(*mid, small_emission)
        return tuple(out[None] for out in outs)

    placed = (
        P("comp", None, "row", "col"),
        P("comp", None, "row", "col"),
        P("comp", "row", "col"),
        P("comp", "row", "col"),
        P("comp", None, "row", "col"),
        P("comp", None, None),
        P("comp", None, None),
        P("comp", "row", "col", None, None),
        P("comp", "row", "col", None),
        P("comp", "row", "col"),
    )
    return jax.shard_map(
        body,
        mesh=mesh,
        in_specs=placed,
        out_specs=(
            P("comp", None, "row", "col"),
            P("comp", None, "row", "col"),
            P("comp", None, "row", "col"),
        ),
        check_vma=False,
    )
```

```python
import functools

import jax
import jax.numpy as jnp
from jax import lax
from jax.experimental import pallas as pl
from jax.experimental.pallas import tpu as pltpu
from jax.sharding import PartitionSpec as P

H = 32
W = 128
K = 4
SPAN = 4
Q = 8
L = 8
SUBSTEPS = 32
FAST = 3
STEP_SIZE = 0.35
DAMPING = 0.97
CHUNKS = 2
PART = 32
ROWS = 3 * H
MESH = pl.DeviceIdType.MESH
TURNS = [(dr, dc) for dr in (-1, 0, 1) for dc in (-1, 0, 1) if (dr, dc) != (0, 0)]


def table_rows(peers):
    return max(16, -(-peers // 16) * 16)


def mask_order(peers):
    bits = peers.bit_length() - 1
    return sorted(range(peers), key=lambda m: int(format(m, "b").zfill(bits)[::-1], 2))


def lower_bits(mask, peers):
    bits = [1 << b for b in reversed(range(peers.bit_length() - 1))]
    return [b for b in bits if mask == 0 or b < (mask & -mask)]


def kernel(peers, bands, *refs):
    remap_kernel(peers, bands, refs[:10], *refs[10:])


def remap_kernel(
    peers,
    bands,
    sources,
    new_column,
    partial,
    wave,
    fixed,
    column,
    fast_state,
    depth,
    wet_mask,
    surface,
    coupling,
    emission,
    weights,
    send_block,
    link_slot,
    mine,
    got,
    table,
    wide,
    turned,
    linked,
    forcing,
    field_a,
    field_e,
    field_w,
    edge_e,
    edge_w,
    push_a,
    push_e,
    push_w,
    pedge_e,
    pedge_w,
    loaded,
    block_send,
    block_recv,
    field_send,
    field_recv,
    push_send,
    push_recv,
):
    comp = lax.axis_index("comp")
    row = lax.axis_index("row")
    col = lax.axis_index("col")
    slots = send_block.shape[1]
    head = table_rows(peers)
    bits = peers.bit_length() - 1
    up_ok = row < bands - 1
    down_ok = row > 0

    def at(dr, dc):
        return {"row": row + dr, "col": lax.rem(col + dc + peers, peers)}

    def reaches(dr):
        return up_ok if dr > 0 else down_ok

    def guarded(dr, act):
        if dr == 0:
            act()
        else:
            pl.when(reaches(dr))(act)

    held = (
        column,
        fast_state,
        depth,
        wet_mask,
        surface,
        coupling,
        emission,
        weights,
        send_block,
        link_slot,
    )

    def load(i):
        return pltpu.make_async_copy(sources[i], held[i], loaded.at[i])

    for i in (4, 3, 8, 1, 2, 7, 9, 5, 0, 6):
        load(i).start()

    barrier = pltpu.get_barrier_semaphore()

    def greet(device):
        pl.semaphore_signal(barrier, inc=1, device_id=device, device_id_type=MESH)

    greet({"comp": 1 - comp})
    for b in range(bits):
        greet({"col": col ^ (1 << b)})
    for dr, dc in TURNS:
        guarded(dr, functools.partial(greet, at(dr, dc)))

    for i in (8, 3, 4):
        load(i).wait()
    wet = wet_mask[...].astype(jnp.float32)
    table[...] = jnp.zeros_like(table)
    table[0:peers, 0:slots] = send_block[...].astype(jnp.float32)
    mine[0:head] = table[...].astype(jnp.bfloat16)
    for q in range(Q):
        mine[head + q * H : head + (q + 1) * H] = (surface[q] * wet).astype(jnp.bfloat16)

    beyond = up_ok.astype(jnp.int32) + down_ok.astype(jnp.int32)
    pl.semaphore_wait(barrier, 1 + bits + 2 + 3 * beyond)

    chunk_rows = Q * H // CHUNKS

    def span_of(chunk):
        if chunk == 0:
            return pl.ds(0, head + chunk_rows)
        return pl.ds(head + chunk * chunk_rows, chunk_rows)

    def block_copy(mask, bit, chunk):
        source = col ^ mask
        index = (mask | bit) * CHUNKS + chunk
        return pltpu.make_async_remote_copy(
            src_ref=got.at[source, span_of(chunk)],
            dst_ref=got.at[source, span_of(chunk)],
            send_sem=block_send.at[index],
            recv_sem=block_recv.at[index],
            device_id={"col": col ^ bit},
            device_id_type=MESH,
        )

    def arrival(mask, chunk):
        source = col ^ mask
        index = mask * CHUNKS + chunk
        if mask == 0:
            return pltpu.make_async_remote_copy(
                src_ref=mine.at[span_of(chunk)],
                dst_ref=got.at[col, span_of(chunk)],
                send_sem=block_send.at[index],
                recv_sem=block_recv.at[index],
                device_id={"comp": 1 - comp},
                device_id_type=MESH,
            )
        bit = mask & -mask
        return pltpu.make_async_remote_copy(
            src_ref=got.at[source, span_of(chunk)],
            dst_ref=got.at[source, span_of(chunk)],
            send_sem=block_send.at[index],
            recv_sem=block_recv.at[index],
            device_id={"col": col ^ bit},
            device_id_type=MESH,
        )

    def halo_copy(dr, dc, middle, east, west, land_e, land_w, send, recv):
        index = TURNS.index((dr, dc))
        land = pl.ds(H - H * dr, H)
        if dc == 0:
            src, dst = middle.at[:, pl.ds(H, H)], middle.at[:, land]
        elif dc > 0:
            src, dst = east, land_w.at[:, land]
        else:
            src, dst = west, land_e.at[:, land]
        return pltpu.make_async_remote_copy(
            src_ref=src,
            dst_ref=dst,
            send_sem=send.at[index],
            recv_sem=recv.at[index],
            device_id=at(dr, dc),
            device_id_type=MESH,
        )

    field_halo = (field_a, edge_e, edge_w, field_e, field_w, field_send, field_recv)
    push_halo = (push_a, pedge_e, pedge_w, push_e, push_w, push_send, push_recv)

    def send_halo(halo, turns):
        for dr, dc in turns:
            guarded(dr, lambda dr=dr, dc=dc: halo_copy(dr, dc, *halo).start())

    def await_halo(halo):
        for dr, dc in TURNS:
            guarded(-dr, lambda dr=dr, dc=dc: halo_copy(dr, dc, *halo).wait_recv())

    def drain_halo(halo):
        for dr, dc in TURNS:
            guarded(dr, lambda dr=dr, dc=dc: halo_copy(dr, dc, *halo).wait_send())

    for chunk in range(CHUNKS):
        arrival(0, chunk).start()

    lane = lax.broadcasted_iota(jnp.int32, (H, W), 1)

    def pack(fields, east, west, tile):
        low = jnp.zeros((H, W), jnp.float32)
        high = jnp.zeros((H, W), jnp.float32)
        for i, cells in enumerate(fields):
            here = (lane >= i * PART) & (lane < (i + 1) * PART)
            first = cells if i == 0 else pltpu.roll(cells, i * PART, 1)
            turn = (i * PART - (W - PART)) % W
            last = cells if turn == 0 else pltpu.roll(cells, turn, 1)
            low = jnp.where(here, first, low)
            high = jnp.where(here, last, high)
        west[tile] = low.astype(west.dtype)
        east[tile] = high.astype(east.dtype)

    own = slice(H, 2 * H)
    for i in (1, 2):
        load(i).wait()
    statics = [fast_state[i] for i in range(FAST)] + [depth[...], wet]
    for i, cells in enumerate(statics):
        field_a[i, own] = cells
    pack(statics[:4], edge_e, edge_w, 0)
    pack(statics[4:], edge_e, edge_w, 1)

    @pl.when(jnp.logical_not(down_ok))
    def _():
        for ref in (field_a, field_e, field_w, push_a, push_e, push_w):
            ref[:, 0:H] = jnp.zeros_like(ref[:, 0:H])

    @pl.when(jnp.logical_not(up_ok))
    def _():
        for ref in (field_a, field_e, field_w, push_a, push_e, push_w):
            ref[:, 2 * H : 3 * H] = jnp.zeros_like(ref[:, 2 * H : 3 * H])

    send_halo(field_halo, TURNS)

    load(7).wait()
    wide[...] = weights[...].astype(jnp.float32)
    for k in range(K):
        for d in range(SPAN):
            plane = wide[pl.ds(k * SPAN + d, H, stride=K * SPAN), :]
            turn = (d - SPAN // 2) % W
            turned[k * SPAN + d] = plane if turn == 0 else pltpu.roll(plane, turn, 1)

    links = H * K
    rows_l = lax.broadcasted_iota(jnp.int32, (links, links), 0)
    lanes_l = lax.broadcasted_iota(jnp.int32, (links, links), 1)

    def hot(condition):
        return jnp.where(condition, 1.0, 0.0).astype(jnp.bfloat16)

    def dot_nt(a, b):
        return lax.dot_general(
            a, b, (((1,), (1,)), ((), ())), preferred_element_type=jnp.float32
        )

    load(9).wait()
    order = hot(lanes_l == (rows_l & (H - 1)) * K + (rows_l >> 5))
    by_slot = hot(rows_l == link_slot[...])
    slot_of_link = dot_nt(order, by_slot).astype(jnp.bfloat16)

    waited = []
    order_of = mask_order(peers)
    senders = [m for m in order_of if m == 0 or lower_bits(m, peers)]
    leaves = [m for m in order_of if m not in senders]

    def receive(mask, chunk):
        arrival(mask, chunk).wait_recv()
        for bit in lower_bits(mask, peers):
            block_copy(mask, bit, chunk).start()

    for mask in senders:
        for chunk in range(CHUNKS):
            receive(mask, chunk)
    pick = None
    per_chunk = Q // CHUNKS
    for chunk in range(CHUNKS):
        for mask in leaves:
            receive(mask, chunk)
        if chunk == 0:
            pieces = []
            rows_h = lax.broadcasted_iota(jnp.int32, (H, W), 0)
            rows_t = lax.broadcasted_iota(jnp.int32, (head, W), 0)
            for s in range(peers):
                listed = got[s, 0:head].astype(jnp.float32)
                chosen = jnp.sum(jnp.where(rows_t == col, listed, 0.0), axis=0, keepdims=True)
                chosen = jnp.broadcast_to(chosen, (H, W)).astype(jnp.int32)
                turn = s * slots % W
                chosen = chosen if turn == 0 else pltpu.roll(chosen, turn, 1)
                here = (lane >= s * slots) & (lane < (s + 1) * slots)
                pieces.append(hot(here & (chosen == rows_h)))
            block_of_slot = jnp.concatenate(pieces, axis=0)
            pick = dot_nt(slot_of_link, block_of_slot).astype(jnp.bfloat16)
        for pair in range(per_chunk // 2):
            first = chunk * per_chunk + 2 * pair
            cells = []
            for q in (first, first + 1):
                tall = got[:, head + q * H : head + (q + 1) * H, :]
                cells.append(tall.reshape(peers * H, W))
            linked[...] = jnp.dot(
                pick, jnp.concatenate(cells, axis=1), preferred_element_type=jnp.float32
            )
            for side in range(2):
                total = jnp.zeros((H, W), jnp.float32)
                for d in range(SPAN):
                    part = jnp.zeros((H, W), jnp.float32)
                    for k in range(K):
                        part = part + (
                            linked[k * H : (k + 1) * H, side * W : (side + 1) * W]
                            * turned[k * SPAN + d]
                        )
                    turn = (SPAN // 2 - d) % W
                    total = total + (part if turn == 0 else pltpu.roll(part, turn, 1))
                forcing[first + side] = total

    load(5).wait()

    def driven(m, rows):
        total = coupling[0, m] * forcing[0, rows]
        for q in range(1, Q):
            total = total + coupling[q, m] * forcing[q, rows]
        return total

    everywhere = slice(0, H)
    pushes = [driven(L + i, everywhere) * (1.0 / SUBSTEPS) for i in range(FAST)]
    for i in range(FAST):
        push_a[i, own] = pushes[i].astype(jnp.bfloat16)
    send_halo(push_halo, [turn for turn in TURNS if turn[1] == 0])
    pack(pushes, pedge_e, pedge_w, 0)
    send_halo(push_halo, [turn for turn in TURNS if turn[1] != 0])

    for i in (0, 6):
        load(i).wait()
    for m in range(L):
        new_column[m] = column[m] + driven(m, everywhere)
    for q in range(Q):
        total = emission[q, 0] * new_column[0]
        for m in range(1, L):
            total = total + emission[q, m] * new_column[m]
        partial[q] = total
    await_halo(field_halo)

    lane_r = lax.broadcasted_iota(jnp.int32, (ROWS, W), 1)

    def beside(east, west, i):
        tile, place = divmod(i, W // PART)
        near = east[tile].astype(jnp.float32)
        near = near if place == 0 else pltpu.roll(near, (W - place * PART) % W, 1)
        turn = (W - PART - place * PART) % W
        far = west[tile].astype(jnp.float32)
        far = far if turn == 0 else pltpu.roll(far, turn, 1)
        cells = jnp.where(lane_r < PART, near, 0.0)
        return jnp.where(lane_r >= W - PART, far, cells)

    scale = [STEP_SIZE, 1.0, 1.0, STEP_SIZE * STEP_SIZE, 1.0]
    for i in range(5):
        ref = wave.at[i] if i < FAST else fixed.at[i - FAST]
        for rows in (slice(0, H), slice(2 * H, ROWS)):
            ref[0, rows] = field_a[i, rows].astype(jnp.float32) * scale[i]
        ref[0, own] = statics[i] * scale[i]
        ref[1] = beside(field_e, field_w, i) * scale[i]
    await_halo(push_halo)
    pscale = [STEP_SIZE, 1.0, 1.0]
    for i in range(FAST):
        for rows in (slice(0, H), slice(2 * H, ROWS)):
            fixed[2 + i, 0, rows] = push_a[i, rows].astype(jnp.float32) * pscale[i]
        fixed[2 + i, 0, own] = pushes[i] * pscale[i]
        fixed[2 + i, 1] = beside(push_e, push_w, i) * pscale[i]

    for chunk in range(CHUNKS):
        for mask in range(peers):
            arrival(mask, chunk).wait_send()
    drain_halo(field_halo)
    drain_halo(push_halo)


def wave_kernel(
    bands,
    new_column,
    partial,
    start,
    fixed,
    emission_source,
    column_out,
    final_out,
    surface_out,
    even,
    odd,
    fast_final,
    next_surface,
    emission,
    sems,
):
    own = slice(H, 2 * H)
    up_ok = lax.axis_index("row") < bands - 1
    load = pltpu.make_async_copy(emission_source, emission, sems.at[0])
    load.start()
    column_copy = pltpu.make_async_copy(new_column, column_out, sems.at[1])
    column_copy.start()
    even[...] = start[...]
    lane8 = lax.broadcasted_iota(jnp.int32, (8, W), 1)
    sub8 = lax.broadcasted_iota(jnp.int32, (8, W), 0)
    west_rim = lane8 == 0
    east_rim = lane8 == W - 1
    south_rim = sub8 == 0
    north_rim = sub8 == 7
    top = jnp.where(up_ok, 1.0, 0.0).astype(jnp.float32)

    def sweep(wave, after, totals, low, high):
        totals = list(totals)
        south_prev = [jnp.zeros((8, W), jnp.float32)] * 2
        held = None
        for block in range(low, high + 2):
            rows = slice(8 * block, 8 * block + 8)
            now = None
            if block <= high:
                flow_e = [wave[1, t, rows] for t in range(2)]
                flow_n = [wave[2, t, rows] for t in range(2)]
                deep = [fixed[0, t, rows] for t in range(2)]
                flux_e = [deep[t] * flow_e[t] for t in range(2)]
                flux_n = [deep[t] * flow_n[t] for t in range(2)]
                spun = [pltpu.roll(flux_e[t], 1, 0 + 1) for t in range(2)]
                lifted = [pltpu.roll(flux_n[t], 1, 0) for t in range(2)]
                high_new = []
                for t in range(2):
                    from_west = jnp.where(west_rim, spun[1 - t], spun[t])
                    from_south = jnp.where(south_rim, south_prev[t], lifted[t])
                    level = (
                        wave[0, t, rows]
                        - ((flux_e[t] - from_west) + (flux_n[t] - from_south))
                        + fixed[2, t, rows]
                    )
                    if block == 2 * H // 8:
                        level = level * top
                    after[0, t, rows] = level
                    high_new.append(level)
                if 4 <= block < 8:
                    totals[block - 4] = totals[block - 4] + high_new[0]
                south_prev = lifted
                down = [pltpu.roll(high_new[t], 7, 0) for t in range(2)]
                now = (rows, block, high_new, flow_e, flow_n, down)
            if held is not None:
                rows, block_h, level, flow_e, flow_n, down = held
                spun = [pltpu.roll(level[t], W - 1, 1) for t in range(2)]
                for t in range(2):
                    to_east = jnp.where(east_rim, spun[1 - t], spun[t])
                    if now is None:
                        to_north = down[t]
                    else:
                        to_north = jnp.where(north_rim, now[5][t], down[t])
                    open_cells = fixed[1, t, rows]
                    east = open_cells * (
                        DAMPING * flow_e[t] - (to_east - level[t]) + fixed[3, t, rows]
                    )
                    north = open_cells * (
                        DAMPING * flow_n[t] - (to_north - level[t]) + fixed[4, t, rows]
                    )
                    after[1, t, rows] = east
                    after[2, t, rows] = north
                    if t == 0 and 4 <= block_h < 8:
                        totals[block_h] = totals[block_h] + east
                        totals[block_h + 4] = totals[block_h + 4] + north
            held = now
        return tuple(totals)

    sums = (jnp.zeros((8, W), jnp.float32),) * (FAST * H // 8)
    for group in range(SUBSTEPS // 8):

        def steps(_, sums, group=group):
            low, high = group, ROWS // 8 - 1 - group
            sums = sweep(even, odd, sums, low, high)
            return sweep(odd, even, sums, low, high)

        sums = lax.fori_loop(0, 4, steps, sums, unroll=2)
    totals = [jnp.concatenate(sums[4 * i : 4 * i + 4], axis=0) for i in range(FAST)]

    back = [1.0 / STEP_SIZE, 1.0, 1.0]
    for i in range(FAST):
        fast_final[i] = even[i, 0, own] * back[i]
    final_copy = pltpu.make_async_copy(fast_final, final_out, sems.at[2])
    final_copy.start()
    load.wait()
    mean = [totals[i] * (back[i] / SUBSTEPS) for i in range(FAST)]
    for q in range(Q):
        total = partial[q]
        for i in range(FAST):
            total = total + emission[q, L + i] * mean[i]
        next_surface[q] = jnp.tanh(total)
    surface_copy = pltpu.make_async_copy(next_surface, surface_out, sems.at[3])
    surface_copy.start()
    surface_copy.wait()
    final_copy.wait()
    column_copy.wait()


def solution(mesh):
    peers = mesh.shape["col"]
    bands = mesh.shape["row"]
    head = table_rows(peers)

    def body(
        column,
        fast_state,
        wave_depth,
        wet_mask,
        surface,
        coupling,
        emission,
        remap_weight,
        send_block,
        link_slot,
    ):
        f32 = jnp.float32
        vmem = pl.BlockSpec(memory_space=pltpu.VMEM)
        hbm = pl.BlockSpec(memory_space=pltpu.HBM)
        dma = pltpu.SemaphoreType.DMA
        small_emission = pltpu.with_memory_space_constraint(emission[0], pltpu.HBM)
        mid = pl.pallas_call(
            functools.partial(kernel, peers, bands),
            out_shape=(
                pltpu.VMEM((L, H, W), f32),
                pltpu.VMEM((Q, H, W), f32),
                pltpu.VMEM((FAST, 2, ROWS, W), f32),
                pltpu.VMEM((5, 2, ROWS, W), f32),
            ),
            in_specs=[hbm] * 10,
            out_specs=(vmem,) * 4,
            scratch_shapes=[
                pltpu.VMEM((L, H, W), f32),
                pltpu.VMEM((FAST, H, W), f32),
                pltpu.VMEM((H, W), f32),
                pltpu.VMEM((H, W), jnp.int32),
                pltpu.VMEM((Q, H, W), f32),
                pltpu.SMEM(coupling.shape[:0:-1], f32),
                pltpu.SMEM(emission.shape[1:], f32),
                pltpu.VMEM((H * K * SPAN, W), jnp.bfloat16),
                pltpu.VMEM(send_block.shape[2:], jnp.int32),
                pltpu.VMEM(link_slot.shape[1:], jnp.int32),
                pltpu.VMEM((head + Q * H, W), jnp.bfloat16),
                pltpu.VMEM((peers, head + Q * H, W), jnp.bfloat16),
                pltpu.VMEM((head, W), f32),
                pltpu.VMEM((H * K * SPAN, W), f32),
                pltpu.VMEM((K * SPAN, H, W), f32),
                pltpu.VMEM((H * K, 2 * W), f32),
                pltpu.VMEM((Q, H, W), f32),
                pltpu.VMEM((5, ROWS, W), f32),
                pltpu.VMEM((2, ROWS, W), f32),
                pltpu.VMEM((2, ROWS, W), f32),
                pltpu.VMEM((2, H, W), f32),
                pltpu.VMEM((2, H, W), f32),
                pltpu.VMEM((FAST, ROWS, W), jnp.bfloat16),
                pltpu.VMEM((1, ROWS, W), jnp.bfloat16),
                pltpu.VMEM((1, ROWS, W), jnp.bfloat16),
                pltpu.VMEM((1, H, W), jnp.bfloat16),
                pltpu.VMEM((1, H, W), jnp.bfloat16),
                dma((10,)),
                dma((peers * CHUNKS,)),
                dma((peers * CHUNKS,)),
                dma((8,)),
                dma((8,)),
                dma((8,)),
                dma((8,)),
            ],
            compiler_params=pltpu.CompilerParams(
                collective_id=0, has_side_effects=True, vmem_limit_bytes=40 << 20
            ),
        )(
*[pltpu.with_memory_space_constraint(x, pltpu.HBM) for x in (column[0],
            fast_state[0],
            wave_depth[0],
            wet_mask[0],
            surface[0],
            coupling[0].T,
            small_emission,
            remap_weight.reshape(H * K * SPAN, W),
            send_block[0, 0],
            link_slot[0],)]
        )
        outs = pl.pallas_call(
            functools.partial(wave_kernel, bands),
            out_shape=(
                jax.ShapeDtypeStruct((L, H, W), f32),
                jax.ShapeDtypeStruct((FAST, H, W), f32),
                jax.ShapeDtypeStruct((Q, H, W), f32),
            ),
            in_specs=[vmem] * 4 + [hbm],
            out_specs=(hbm,) * 3,
            scratch_shapes=[
                pltpu.VMEM((FAST, 2, ROWS, W), f32),
                pltpu.VMEM((FAST, 2, ROWS, W), f32),
                pltpu.VMEM((FAST, H, W), f32),
                pltpu.VMEM((Q, H, W), f32),
                pltpu.SMEM(emission.shape[1:], f32),
                dma((4,)),
            ],
            compiler_params=pltpu.CompilerParams(vmem_limit_bytes=16 << 20),
        )(*mid, small_emission)
        return tuple(out[None] for out in outs)

    placed = (
        P("comp", None, "row", "col"),
        P("comp", None, "row", "col"),
        P("comp", "row", "col"),
        P("comp", "row", "col"),
        P("comp", None, "row", "col"),
        P("comp", None, None),
        P("comp", None, None),
        P("comp", "row", "col", None, None),
        P("comp", "row", "col", None),
        P("comp", "row", "col"),
    )
    return jax.shard_map(
        body,
        mesh=mesh,
        in_specs=placed,
        out_specs=(
            P("comp", None, "row", "col"),
            P("comp", None, "row", "col"),
            P("comp", None, "row", "col"),
        ),
        check_vma=False,
    )
```
